256 devices in a mesh: sn: 16 (over y_hi, x, core), pan: 16 (over y_lo, z).
Axes of the slice: x: 4, y: 4 (y_hi: 2, y_lo: 2; y = y_hi * 2 + y_lo), z: 8, core: 2. Of those that a mesh axis runs over, the one named last changes fastest.
Arguments:
- pattern: int32 [6, 10, 64], replicated, may hold values 0 or 1
- pivot_root: float32 [512, 512], P('pan', 'sn'), may hold values from -1 to 5, as said below
- pivot_first: float32 [512, 1024], P('pan', 'sn'), may hold values from -1 to 5, as said below
- factor_first: float32 [1, 512, 1024], P(None, 'pan', 'sn'), may hold values from -0.078125 to 0.078125
- pivot_second: float32 [512, 2048], P('pan', 'sn'), may hold values from -1 to 5, as said below
- factor_second: float32 [2, 512, 2048], P(None, 'pan', 'sn'), may hold values from -0.078125 to 0.078125
- pivot_third: float32 [512, 4096], P('pan', 'sn'), may hold values from -1 to 5, as said below
- factor_third: float32 [3, 512, 4096], P(None, 'pan', 'sn'), may hold values from -0.078125 to 0.078125
- pivot_fourth: float32 [512, 8192], P('pan', 'sn'), may hold values from -1 to 5, as said below
- factor_fourth: float32 [4, 512, 8192], P(None, 'pan', 'sn'), may hold values from -0.078125 to 0.078125
- pivot_leaves: float32 [512, 16384], P('pan', 'sn'), may hold values from -1 to 5, as said below
- factor_leaves: float32 [5, 512, 16384], P(None, 'pan', 'sn'), may hold values from -0.078125 to 0.078125
Outputs:
- pair_blocks: float32 [5, 512, 16384], P(None, 'pan', 'sn')
- self_blocks: float32 [512, 16384], P('pan', 'sn')
The draws below stay inside these ranges and needn't reach their ends.
Inputs may be any that keep to these rules, and one draw needn't show every extreme that they name: `pivot_root`: each 512 x 512 node block is symmetric. `pivot_first`: each 512 x 512 node block is symmetric. `pivot_second`: each 512 x 512 node block is symmetric. `pivot_third`: each 512 x 512 node block is symmetric. `pivot_fourth`: each 512 x 512 node block is symmetric. `pivot_leaves`: each 512 x 512 node block is symmetric.
All inputs are finite; a program needn't handle non-finite values.
Results may differ from the reference program's by a relative error of at most 0.0003.
Values sent between devices are 32-bit elements; how exact they have to be, the bound alone decides.
No kernel may reach another device: no remote copies, remote signals or barrier semaphores. Data moves between devices by JAX's collectives and lax.ppermute only.
A program may use at most 128 MiB of HBM per device.

```python
import math
import jax
import jax.numpy as jnp
from jax import lax

W = 256
SUPERS = 2
LEVELS = 6
NW = 512
LEAVES = 32


def assemble(diag_values, off_values, number):
    scale = 0.25 / NW ** 0.5
    symmetric = (off_values + off_values.transpose(0, 2, 1)) * scale
    identity = (jnp.arange(NW)[:, None] == jnp.arange(NW)[None, :]).astype(jnp.float32)
    result = symmetric + identity[None] * diag_values[:, :, None]
    return result.transpose(1, 0, 2).reshape(NW, number * NW)


def drawn_parts(key, number):
    key_diag, key_off = jax.random.split(key)
    diag_values = jnp.exp(jax.random.uniform(key_diag, (number, NW), jnp.float32, 0.0, math.log(4.0)))
    off_values = jnp.clip(jax.random.normal(key_off, (number, NW, NW), jnp.float32), -4.0, 4.0)
    return (diag_values, off_values)


def draw_pivot_root(key, part):
    key = jax.random.fold_in(key, 11)
    diag_values, off_values = drawn_parts(key, 1)
    return assemble(diag_values, off_values, 1)


def draw_pivot_first(key, part):
    key = jax.random.fold_in(key, 12)
    diag_values, off_values = drawn_parts(key, 2)
    return assemble(diag_values, off_values, 2)


def draw_pivot_second(key, part):
    key = jax.random.fold_in(key, 13)
    diag_values, off_values = drawn_parts(key, 4)
    return assemble(diag_values, off_values, 4)


def draw_pivot_third(key, part):
    key = jax.random.fold_in(key, 14)
    diag_values, off_values = drawn_parts(key, 8)
    return assemble(diag_values, off_values, 8)


def draw_pivot_fourth(key, part):
    key = jax.random.fold_in(key, 15)
    diag_values, off_values = drawn_parts(key, 16)
    return assemble(diag_values, off_values, 16)


def draw_pivot_leaves(key, part):
    key = jax.random.fold_in(key, 16)
    diag_values, off_values = drawn_parts(key, LEAVES)
    return assemble(diag_values, off_values, LEAVES)


def plant(values, rng, low, high):
    extent = values.shape
    spot = [jax.random.randint(jax.random.fold_in(rng, axis), (), 0, extent[axis]) for axis in range(len(extent))]
    values = values.at[tuple(spot)].set(low)
    longest = extent.index(max(extent))
    spot[longest] = (spot[longest] + 1) % extent[longest]
    return values.at[tuple(spot)].set(high)


def shard_levels(stream_key, dims, pieces, least, largest):
    loudness = 1.0
    for position, parts in pieces:
        steps = jax.random.uniform(jax.random.fold_in(jax.random.fold_in(stream_key, 6), position), (parts,), jnp.float32, least / len(pieces), largest / len(pieces))
        loudness = loudness * jnp.repeat(jnp.exp(steps), dims[position] // parts).reshape((-1,) + (1,) * (len(dims) - 1 - position))
    return loudness


def centred(key, extent, deviation, limit, shards=(), kind=jnp.bfloat16):
    values = jax.random.normal(key, extent, jnp.float32) * deviation
    if len(shards) > 0:
        values = shard_levels(key, extent, shards, -0.22, 0.18) * values
    return jnp.clip(values, min=-limit, max=limit).astype(kind)


def setup_inputs(seed: int = 0) -> dict:
    splits = jax.random.split(jax.random.key(seed), 13)
    return {
        "pattern": plant((jax.random.randint(splits[0], (LEVELS, (LEVELS - 1) * SUPERS, LEAVES * SUPERS), 0, 4) < 3).astype(jnp.int32), jax.random.fold_in(splits[0], 1), 0, 1),
        "pivot_root": draw_pivot_root(jax.random.fold_in(splits[12], 71), 0),
        "pivot_first": draw_pivot_first(jax.random.fold_in(splits[12], 71), 0),
        "factor_first": centred(splits[3], (1, NW, 2 * NW), (0.13 / NW ** 0.5), 0.078125, ((1, 16), (2, 16)), jnp.float32),
        "pivot_second": draw_pivot_second(jax.random.fold_in(splits[12], 71), 0),
        "factor_second": centred(splits[5], (2, NW, 4 * NW), (0.13 / NW ** 0.5), 0.078125, ((1, 16), (2, 16)), jnp.float32),
        "pivot_third": draw_pivot_third(jax.random.fold_in(splits[12], 71), 0),
        "factor_third": centred(splits[7], (3, NW, 8 * NW), (0.13 / NW ** 0.5), 0.078125, ((1, 16), (2, 16)), jnp.float32),
        "pivot_fourth": draw_pivot_fourth(jax.random.fold_in(splits[12], 71), 0),
        "factor_fourth": centred(splits[9], (4, NW, 16 * NW), (0.13 / NW ** 0.5), 0.078125, ((1, 16), (2, 16)), jnp.float32),
        "pivot_leaves": draw_pivot_leaves(jax.random.fold_in(splits[12], 71), 0),
        "factor_leaves": centred(splits[11], (LEVELS - 1, NW, LEAVES * NW), (0.13 / NW ** 0.5), 0.078125, ((1, 16), (2, 16)), jnp.float32),
    }


exact_mode = lax.Precision.HIGHEST


def level_mask(pattern, level_num):
    number = 2 ** level_num
    pattern_cut = pattern[level_num, :level_num * SUPERS, :number * SUPERS]
    spread = jnp.repeat(jnp.repeat(pattern_cut, W, axis=0), W, axis=1)
    return spread.astype(jnp.float32).reshape(level_num, NW, number * NW)


def reference(pattern, pivot_root, pivot_first, factor_first, pivot_second, factor_second, pivot_third, factor_third, pivot_fourth, factor_fourth, pivot_leaves, factor_leaves):
    pivots = [pivot_root, pivot_first, pivot_second, pivot_third, pivot_fourth, pivot_leaves]
    factors = [pivot_root, factor_first, factor_second, factor_third, factor_fourth, factor_leaves]
    ancestry = pivot_root[None]
    columns = None
    self_list = None
    for level_num in range(1, LEVELS):
        number = 2 ** level_num
        masked = factors[level_num] * level_mask(pattern, level_num)
        panels = masked.reshape(level_num * NW, number, NW).transpose(1, 0, 2)
        blocks = pivots[level_num].reshape(NW, number, NW).transpose(1, 0, 2)
        previous = ancestry

        def solve_node(node_index, previous=previous, panels=panels, blocks=blocks):
            parent = lax.dynamic_index_in_dim(previous, node_index // 2, 0, keepdims=False)
            panel_cols = lax.dynamic_index_in_dim(panels, node_index, 0, keepdims=False)
            pivot_block = lax.dynamic_index_in_dim(blocks, node_index, 0, keepdims=False)
            column = -jnp.dot(parent, panel_cols, precision=exact_mode)
            self_block = pivot_block - jnp.dot(panel_cols.T, column, precision=exact_mode)
            return column, self_block

        columns, self_list = lax.map(solve_node, jnp.arange(number, dtype=jnp.int32))
        if level_num < LEVELS - 1:
            def extend(node_index, previous=previous, columns=columns, self_list=self_list):
                parent = lax.dynamic_index_in_dim(previous, node_index // 2, 0, keepdims=False)
                column = lax.dynamic_index_in_dim(columns, node_index, 0, keepdims=False)
                self_block = lax.dynamic_index_in_dim(self_list, node_index, 0, keepdims=False)
                upper_rows = jnp.concatenate([parent, column], axis=1)
                lower_rows = jnp.concatenate([column.T, self_block], axis=1)
                return jnp.concatenate([upper_rows, lower_rows], axis=0)

            ancestry = lax.map(extend, jnp.arange(number, dtype=jnp.int32))
    last = LEVELS - 1
    pair_blocks = columns.reshape(LEAVES, last, NW, NW).transpose(1, 2, 0, 3).reshape(last, NW, LEAVES * NW)
    self_blocks = self_list.transpose(1, 0, 2).reshape(NW, LEAVES * NW)
    return pair_blocks, self_blocks
```

```python
import jax
import jax.numpy as jnp
from jax import lax
from jax.sharding import PartitionSpec as P

W = 256
SUPERS = 2
NW = 512
ROWS = 32
RING = 8

three_pass = lax.Precision.HIGH


def place(index):
    sn, pan = divmod(index, 16)
    y_hi, rest = divmod(sn, 8)
    x, core = divmod(rest, 2)
    y_lo, z = divmod(pan, RING)
    return y_hi, x, core, y_lo, z


def number(y_hi, x, core, y_lo, z):
    return (y_hi * 8 + x * 2 + core) * 16 + y_lo * RING + z


def route(move):
    pairs = []
    for index in range(256):
        target = number(*move(*place(index)))
        if target != index:
            pairs.append((index, target))
    return pairs


CORE = route(lambda yh, x, c, yl, z: (yh, x, 1 - c, yl, z))
X_LOW = route(lambda yh, x, c, yl, z: (yh, x ^ 1, c, yl, z))
X_HIGH = route(lambda yh, x, c, yl, z: (yh, x ^ 2, c, yl, z))
Y_HIGH = route(lambda yh, x, c, yl, z: (1 - yh, x, c, yl, z))
Y_LOW = route(lambda yh, x, c, yl, z: (yh, x, c, 1 - yl, z))
TURN = route(lambda yh, x, c, yl, z: (yh, x, yl, c, z))
Z_UP = route(lambda yh, x, c, yl, z: (yh, x, c, yl, (z + 1) % RING))
Z_DOWN = route(lambda yh, x, c, yl, z: (yh, x, c, yl, (z - 1) % RING))


def send(block, pairs):
    return lax.ppermute(block, ("sn", "pan"), pairs)


def join(block, pairs, bit):
    other = send(block, pairs)
    return jnp.where(
        bit == 1,
        jnp.concatenate([other, block], axis=-1),
        jnp.concatenate([block, other], axis=-1),
    )


def ring_gather(shard, z):
    half = shard.shape[0] // 2
    up, down = shard, shard
    found = [(0, shard)]
    for step in range(1, 4):
        up = send(up, Z_UP)
        down = send(down, Z_DOWN)
        found += [(-step, up), (step, down)]
    far = jnp.concatenate([send(up[:half], Z_UP), send(down[half:], Z_DOWN)], axis=0)
    found.append((4, far))
    whole = jnp.zeros((RING,) + shard.shape, shard.dtype)
    for offset, block in found:
        whole = lax.dynamic_update_index_in_dim(whole, block, (z + offset) % RING, 0)
    return whole


def masked(factor, pattern, level, sn, y_lo):
    depth, rows, cols = factor.shape
    count = max(1, cols // W)
    first = sn * cols // W
    rows_cut = pattern[level, : depth * SUPERS].reshape(depth, SUPERS, -1)
    cut = lax.dynamic_slice(rows_cut, (0, y_lo, first), (depth, 1, count))
    spread = cut.astype(jnp.float32).reshape(depth, 1, count, 1)
    return (factor.reshape(depth, rows, count, cols // count) * spread).reshape(factor.shape)


def times(left, right):
    return lax.dot_general(
        left, right, (((1,), (0,)), ((), ())), precision=three_pass,
        preferred_element_type=jnp.float32,
    )


def times_turned(left, right):
    return lax.dot_general(
        left, right, (((1,), (1,)), ((), ())), precision=three_pass,
        preferred_element_type=jnp.float32,
    )


def sweep(parts, panels, pivots, unit=None):
    parts = list(parts)
    top = len(parts) - 1
    for level in range(top, -1, -1):
        if unit is not None:
            known = [] if parts[level] is None else [parts[level]]
            parts[level] = jnp.concatenate(known + [unit], axis=0)
        if level == 0:
            break
        moved = times_turned(parts[level], panels[level].reshape(level * NW, NW))
        for above in range(level):
            piece = moved[:, above * NW : (above + 1) * NW]
            if parts[above] is None:
                parts[above] = -piece
            else:
                held = parts[above].shape[0]
                parts[above] = jnp.concatenate([parts[above] - piece[:held], -piece[held:]], 0)
    done = [times(part, pivots[level]) for level, part in enumerate(parts)]
    for level in range(1, top + 1):
        moved = times(
            jnp.concatenate(done[:level], axis=1), panels[level].reshape(level * NW, NW)
        )
        lacking = moved.shape[0] - done[level].shape[0]
        done[level] = jnp.pad(done[level], ((0, lacking), (0, 0))) - moved
    return done


def per_device(
    pattern,
    pivot_root,
    pivot_first,
    factor_first,
    pivot_second,
    factor_second,
    pivot_third,
    factor_third,
    pivot_fourth,
    factor_fourth,
    pivot_leaves,
    factor_leaves,
):
    sn = lax.axis_index("sn")
    pan = lax.axis_index("pan")
    core = sn % 2
    x_low = sn // 2 % 2
    x_high = sn // 4 % 2
    y_high = sn // 8
    y_lo = pan // RING
    z = pan % RING
    mine = core * RING + z

    third = jnp.concatenate([masked(factor_third, pattern, 3, sn, y_lo), pivot_third[None]], 0)
    second = jnp.concatenate([masked(factor_second, pattern, 2, sn, y_lo), pivot_second[None]], 0)
    first = jnp.concatenate([masked(factor_first, pattern, 1, sn, y_lo), pivot_first[None]], 0)
    root = pivot_root[None]
    fourth = jnp.concatenate([masked(factor_fourth, pattern, 4, sn, y_lo), pivot_fourth[None]], 0)
    leaves = masked(factor_leaves, pattern, 5, sn, y_lo)

    own = core == y_lo
    fourth = jnp.where(own, fourth, send(fourth, TURN))
    leaves = jnp.where(own, leaves, send(leaves, TURN))

    third = join(third, CORE, core)
    second = join(second, CORE, core)
    first = join(first, CORE, core)
    root = join(root, CORE, core)
    second = join(second, X_LOW, x_low)
    first = join(first, X_LOW, x_low)
    root = join(root, X_LOW, x_low)
    first = join(first, X_HIGH, x_high)
    root = join(root, X_HIGH, x_high)
    root = join(root, Y_HIGH, y_high)
    upper = jnp.concatenate([third, second, first, root], axis=0)
    upper = lax.dynamic_slice_in_dim(upper, core * W, W, 2)
    other = send(upper, Y_LOW)
    upper = jnp.where(
        y_lo == 1, jnp.stack([other, upper], 1), jnp.stack([upper, other], 1)
    )

    upper = ring_gather(upper, z)
    fourth = ring_gather(fourth, z)
    leaves = ring_gather(leaves, z)

    upper_other = send(upper, CORE)
    upper = jnp.where(
        core == 1,
        jnp.concatenate([upper_other, upper], axis=-1),
        jnp.concatenate([upper, upper_other], axis=-1),
    )
    upper = upper.transpose(1, 2, 0, 3, 4).reshape(10, NW, NW)
    fourth_other = send(fourth, CORE)
    fourth = jnp.where(
        core == 1, jnp.stack([fourth_other, fourth]), jnp.stack([fourth, fourth_other])
    )
    fourth = fourth.transpose(2, 0, 1, 3, 4).reshape(5, NW, NW)
    panels = [None, upper[7:8], upper[4:6], upper[0:3], fourth[0:4]]
    pivots = [upper[9], upper[8], upper[6], upper[3], fourth[4]]

    unit = (
        mine * ROWS + jnp.arange(ROWS, dtype=jnp.int32)[:, None]
        == jnp.arange(NW, dtype=jnp.int32)[None, :]
    ).astype(jnp.float32)
    path = sweep([None] * 5, panels, pivots, unit)

    sides = leaves.reshape(RING * 5 * ROWS, 2, 2 * RING, ROWS)
    wanted = lax.dynamic_index_in_dim(sides, mine, 2, keepdims=False)
    theirs = lax.dynamic_index_in_dim(sides, (1 - core) * RING + z, 2, keepdims=False)
    got = send(theirs.reshape(RING * 5 * ROWS, 2 * ROWS), CORE)
    wanted = wanted.reshape(RING * 5 * ROWS, 2 * ROWS)
    both = jnp.where(core == 1, jnp.stack([got, wanted]), jnp.stack([wanted, got]))
    both = both.reshape(2, RING, 5, ROWS, 2 * ROWS).transpose(2, 4, 0, 1, 3).reshape(5, 2 * ROWS, NW)
    self_path = sweep([both[level] for level in range(5)], panels, pivots)

    left = jnp.concatenate(
        [jnp.stack(path, 1), jnp.stack(self_path, 1)], axis=0
    ).reshape(7 * ROWS, 5, 2, RING, ROWS)
    keep = lax.dynamic_index_in_dim(left, core, 2, keepdims=False)
    give = lax.dynamic_index_in_dim(left, 1 - core, 2, keepdims=False)
    taken = send(give, CORE)
    left = jnp.concatenate([keep, taken], 0).transpose(0, 2, 1, 3).reshape(14 * ROWS, RING * 5 * ROWS)
    right = leaves.reshape(RING * 5 * ROWS, 2 * NW)
    total = times(left, right).reshape(2, 7 * ROWS, 2 * NW)
    total = total[0] + send(total[1], CORE)
    pair_rows = total[: 5 * ROWS].reshape(5, ROWS, 2 * NW)[::-1]
    self_rows = total[5 * ROWS :].reshape(2, ROWS, 2, NW)
    self_rows = jnp.concatenate([self_rows[0, :, 0], self_rows[1, :, 1]], axis=-1)
    out = jnp.concatenate([-pair_rows, self_rows[None]], 0)
    out = jnp.where(own, out, send(out, TURN))
    return out[:5], pivot_leaves + out[5]


def solution(mesh):
    tree = P("pan", "sn")
    panel = P(None, "pan", "sn")
    return jax.shard_map(
        per_device,
        mesh=mesh,
        in_specs=(P(), tree, tree, panel, tree, panel, tree, panel, tree, panel, tree, panel),
        out_specs=(panel, tree),
        check_vma=False,
    )
```

```python
import jax
import jax.numpy as jnp
from jax import lax
from jax.experimental import pallas as pl
from jax.experimental.pallas import tpu as pltpu
from jax.sharding import PartitionSpec as P

W = 256
SUPERS = 2
NW = 512
ROWS = 32
RING = 8
FIRST_BLOCK = {1: 3, 2: 0, 3: 6, 4: 10}
PIVOT_BLOCK = {0: 5, 1: 4, 2: 2, 3: 9, 4: 14}
VMEM_BYTES = 52 * 1024 * 1024

def place(index):
    sn, pan = divmod(index, 16)
    y_hi, rest = divmod(sn, 8)
    x, core = divmod(rest, 2)
    y_lo, z = divmod(pan, RING)
    return y_hi, x, core, y_lo, z


def number(y_hi, x, core, y_lo, z):
    return (y_hi * 8 + x * 2 + core) * 16 + y_lo * RING + z


def route(move):
    pairs = []
    for index in range(256):
        target = number(*move(*place(index)))
        if target != index:
            pairs.append((index, target))
    return pairs


CORE = route(lambda yh, x, c, yl, z: (yh, x, 1 - c, yl, z))
X_LOW = route(lambda yh, x, c, yl, z: (yh, x ^ 1, c, yl, z))
X_HIGH = route(lambda yh, x, c, yl, z: (yh, x ^ 2, c, yl, z))
Y_HIGH = route(lambda yh, x, c, yl, z: (1 - yh, x, c, yl, z))
Y_LOW = route(lambda yh, x, c, yl, z: (yh, x, c, 1 - yl, z))
TURN = route(lambda yh, x, c, yl, z: (yh, x, yl, c, z))
Z_BOTH = route(lambda yh, x, c, yl, z: (yh, x, c, yl, (z + 1 - 2 * c) % RING))


def send(block, pairs):
    return lax.ppermute(block, ("sn", "pan"), pairs)


def join(block, pairs, bit):
    other = send(block, pairs)
    return jnp.where(
        bit == 1,
        jnp.concatenate([other, block], axis=-1),
        jnp.concatenate([block, other], axis=-1),
    )


def ring(shard, core):
    found = []
    held = shard
    for step in range(3):
        held = send(held, Z_BOTH)
        found.append(held)
    far = send(lax.dynamic_index_in_dim(held, core, 0, keepdims=False), Z_BOTH)
    return found, far


def ordered(mine, other, core):
    return jnp.where(core == 0, jnp.stack([mine, other]), jnp.stack([other, mine]))


def position():
    sn = lax.axis_index("sn")
    pan = lax.axis_index("pan")
    return sn % 2, sn // 2 % 2, pan // RING, pan % RING


def mask_kernel(pattern, *refs):
    sn = lax.axis_index("sn")
    y_lo = lax.axis_index("pan") // RING
    ins, outs = refs[:9], refs[9:]
    for level in range(1, 6):
        factor, out = ins[level - 1], outs[level - 1]
        cols = factor.shape[2]
        count = max(1, cols // W)
        width = cols // count
        for above in range(level):
            for part in range(count):
                scale = pattern[level, above * SUPERS + y_lo, sn * cols // W + part]
                span = slice(part * width, (part + 1) * width)
                out[above, :, span] = factor[above, :, span] * scale.astype(jnp.float32)
        if level < 5:
            out[level] = ins[4 + level][...]


def mask_all(pattern, factors, pivots):
    shapes = [
        jax.ShapeDtypeStruct((f.shape[0] + (f.shape[0] < 5),) + f.shape[1:], jnp.float32)
        for f in factors
    ]
    vmem = pl.BlockSpec(memory_space=pltpu.VMEM)
    return pl.pallas_call(
        mask_kernel,
        out_shape=shapes,
        in_specs=[pl.BlockSpec(memory_space=pltpu.SMEM)] + [vmem] * 9,
        out_specs=[vmem] * 5,
    )(pattern, *factors, *pivots)


def split(value):
    high = value.astype(jnp.bfloat16)
    return high, (value - high.astype(jnp.float32)).astype(jnp.bfloat16)


def product(left, right, turned):
    dims = (((1,), (1 if turned else 0,)), ((), ()))
    return lax.dot_general(left, right, dims, preferred_element_type=jnp.float32)


def triple(pair, high, low, turned):
    rows = pair[0].shape[0]
    both = product(jnp.concatenate(pair, axis=0), high, turned)
    return both[:rows] + both[rows:] + product(pair[0], low, turned)


def sweep(parts, high, low, unit, ready):
    parts = list(parts)
    for level in range(4, -1, -1):
        if unit is not None:
            known = [] if parts[level] is None else [parts[level]]
            parts[level] = jnp.concatenate(known + [unit], axis=0)
        if level == 0:
            break
        ready(level)
        pair = split(parts[level])
        for above in range(level):
            block = FIRST_BLOCK[level] + above
            piece = triple(pair, high[block], low[block], True)
            if parts[above] is None:
                parts[above] = -piece
            else:
                held = parts[above].shape[0]
                if held == piece.shape[0]:
                    parts[above] = parts[above] - piece
                else:
                    parts[above] = jnp.concatenate([parts[above] - piece[:held], -piece[held:]], 0)
    ready(0)
    done = [
        triple(split(part), high[PIVOT_BLOCK[level]], low[PIVOT_BLOCK[level]], False)
        for level, part in enumerate(parts)
    ]
    pairs = [split(done[0])]
    for level in range(1, 5):
        total = None
        for above in range(level):
            block = FIRST_BLOCK[level] + above
            term = triple(pairs[above], high[block], low[block], False)
            total = term if total is None else total + term
        held = done[level].shape[0]
        if held == total.shape[0]:
            done[level] = done[level] - total
        else:
            done[level] = jnp.concatenate([done[level] - total[:held], -total[held:]], axis=0)
        pairs.append(split(done[level]))
    return done, pairs


def whole_wait(ref, sem):
    pltpu.make_async_copy(ref, ref, sem).wait()


def path_kernel(*refs):
    (fourth_own, f1, f2, f3, g1, g2, g3, f_far, g_far), refs = refs[:9], refs[9:]
    lower, third = refs[:8], refs[8:12]
    rows_out, high_out, low_out = refs[12:15]
    raw, high, low, in_sem, out_sem = refs[15:]
    core, x_low, y_lo, z = position()
    mine = core * RING + z

    def copy(source, first, count, row, lane, width, sem):
        row = pl.multiple_of(row * ROWS, ROWS)
        if not isinstance(lane, int):
            lane = pl.multiple_of(lane, W)
        pltpu.make_async_copy(
            source, raw.at[pl.ds(first, count), pl.ds(row, ROWS), pl.ds(lane, width)], in_sem.at[sem]
        ).start()

    def turn(step, own):
        sign = 2 * core - 1 if own else 1 - 2 * core
        return lax.rem(z + sign * step + RING, RING)

    def side(own):
        return core if own else 1 - core

    far_z = lax.rem(z + 4, RING)
    for half in range(2):
        copy(fourth_own.at[half], 10, 5, half * RING + z, 0, NW, 0)
        for step, (a, b) in enumerate(((f1, g1), (f2, g2), (f3, g3)), 1):
            copy(a.at[half], 10, 5, half * RING + turn(step, True), 0, NW, 0)
            copy(b.at[half], 10, 5, half * RING + turn(step, False), 0, NW, 0)
    copy(f_far, 10, 5, side(True) * RING + far_z, 0, NW, 0)
    copy(g_far, 10, 5, side(False) * RING + far_z, 0, NW, 0)

    for index, source in enumerate(third):
        flip, own = index // 2, index % 2 == 0
        base = (y_lo if flip == 0 else 1 - y_lo) * RING
        for step in range(3):
            for half in range(2):
                copy(source.at[step, half], 6, 4, base + turn(step + 1, own), half * W, W, 1)
        copy(source.at[3, 0], 6, 4, base + z, side(own) * W, W, 1)
        copy(source.at[3, 1], 6, 4, base + far_z, side(own) * W, W, 1)

    for index, source in enumerate(lower):
        flip, own = index // 2, index % 2 == 0
        base = (y_lo if flip // 2 == 0 else 1 - y_lo) * RING
        lane = (x_low if flip % 2 == 0 else 1 - x_low) * W
        for step in range(3):
            for half in range(2):
                copy(source.at[step, half], half * 3, 3, base + turn(step + 1, own), lane, W, 2)
        copy(source.at[3, 0], side(own) * 3, 3, base + z, lane, W, 2)
        copy(source.at[3, 1], side(own) * 3, 3, base + far_z, lane, W, 2)

    def take(first, count, sem):
        whole_wait(raw.at[pl.ds(first, count)], in_sem.at[sem])

        def one(block, carry):
            high[block], low[block] = split(raw[block])
            return carry

        lax.fori_loop(first, first + count, one, 0)
        span = pl.ds(first, count)
        pltpu.make_async_copy(high.at[span], high_out.at[span], out_sem.at[2 * sem]).start()
        pltpu.make_async_copy(low.at[span], low_out.at[span], out_sem.at[2 * sem + 1]).start()

    def ready(level):
        if level == 4:
            take(10, 5, 0)
        if level == 3:
            take(6, 4, 1)
        if level == 2:
            take(0, 6, 2)

    unit = (
        mine * ROWS + lax.broadcasted_iota(jnp.int32, (ROWS, NW), 0)
        == lax.broadcasted_iota(jnp.int32, (ROWS, NW), 1)
    ).astype(jnp.float32)
    done, _ = sweep([None] * 5, high, low, unit, ready)
    for level in range(5):
        rows_out[:, level * NW : (level + 1) * NW] = done[level]
    for sem, (first, count) in enumerate(((10, 5), (6, 4), (0, 6))):
        span = pl.ds(first, count)
        pltpu.make_async_copy(high.at[span], high_out.at[span], out_sem.at[2 * sem]).wait()
        pltpu.make_async_copy(low.at[span], low_out.at[span], out_sem.at[2 * sem + 1]).wait()


def path_rows(fourth, lower, third):
    held = jax.ShapeDtypeStruct((15, NW, NW), jnp.bfloat16)
    count = 9 + len(lower) + len(third)
    return pl.pallas_call(
        path_kernel,
        out_shape=[jax.ShapeDtypeStruct((5 * ROWS, 5 * NW), jnp.float32), held, held],
        in_specs=[pl.BlockSpec(memory_space=pl.ANY)] * count,
        out_specs=[
            pl.BlockSpec(memory_space=pltpu.VMEM),
            pl.BlockSpec(memory_space=pl.ANY),
            pl.BlockSpec(memory_space=pl.ANY),
        ],
        scratch_shapes=[
            pltpu.VMEM((15, NW, NW), jnp.float32),
            pltpu.VMEM((15, NW, NW), jnp.bfloat16),
            pltpu.VMEM((15, NW, NW), jnp.bfloat16),
            pltpu.SemaphoreType.DMA((3,)),
            pltpu.SemaphoreType.DMA((6,)),
        ],
        compiler_params=pltpu.CompilerParams(vmem_limit_bytes=VMEM_BYTES),
    )(*fourth, *lower, *third)


def pair_kernel(rows, own_shard, f1, f2, f3, g1, g2, g3, f_far, g_far, out, high_out, low_out, raw, high, low, in_sem, out_sem):
    core, _, _, z = position()
    far_z = lax.rem(z + 4, RING)

    def turn(step, own):
        sign = 2 * core - 1 if own else 1 - 2 * core
        return lax.rem(z + sign * step + RING, RING)

    for level in range(5):

        def copy(source, row):
            row = pl.multiple_of(row * ROWS, ROWS)
            pltpu.make_async_copy(source, raw.at[level, pl.ds(row, ROWS)], in_sem.at[level]).start()

        for half in range(2):
            copy(own_shard.at[half, level], half * RING + z)
            for step, (a, b) in enumerate(((f1, g1), (f2, g2), (f3, g3)), 1):
                copy(a.at[half, level], half * RING + turn(step, True))
                copy(b.at[half, level], half * RING + turn(step, False))
        copy(f_far.at[level], core * RING + far_z)
        copy(g_far.at[level], (1 - core) * RING + far_z)

    total = None
    for level in range(5):
        whole_wait(raw.at[level], in_sem.at[level])
        for part in range(2):
            span = slice(part * NW, (part + 1) * NW)
            high[level, :, span], low[level, :, span] = split(raw[level, :, span])
        pltpu.make_async_copy(high.at[level], high_out.at[level], out_sem.at[level, 0]).start()
        pltpu.make_async_copy(low.at[level], low_out.at[level], out_sem.at[level, 1]).start()
        pair = split(rows[:, level * NW : (level + 1) * NW])
        term = triple(pair, high[level], low[level], False)
        total = term if total is None else total + term
    for level in range(5):
        first = (4 - level) * ROWS
        out[level] = -total[first : first + ROWS]
    for level in range(5):
        pltpu.make_async_copy(high.at[level], high_out.at[level], out_sem.at[level, 0]).wait()
        pltpu.make_async_copy(low.at[level], low_out.at[level], out_sem.at[level, 1]).wait()


def pair_rows(rows, pieces):
    held = jax.ShapeDtypeStruct((5, NW, 2 * NW), jnp.bfloat16)
    return pl.pallas_call(
        pair_kernel,
        out_shape=[jax.ShapeDtypeStruct((5, ROWS, 2 * NW), jnp.float32), held, held],
        in_specs=[pl.BlockSpec(memory_space=pltpu.VMEM)] + [pl.BlockSpec(memory_space=pl.ANY)] * 9,
        out_specs=[
            pl.BlockSpec(memory_space=pltpu.VMEM),
            pl.BlockSpec(memory_space=pl.ANY),
            pl.BlockSpec(memory_space=pl.ANY),
        ],
        scratch_shapes=[
            pltpu.VMEM((5, NW, 2 * NW), jnp.float32),
            pltpu.VMEM((5, NW, 2 * NW), jnp.bfloat16),
            pltpu.VMEM((5, NW, 2 * NW), jnp.bfloat16),
            pltpu.SemaphoreType.DMA((5,)),
            pltpu.SemaphoreType.DMA((5, 2)),
        ],
        compiler_params=pltpu.CompilerParams(vmem_limit_bytes=VMEM_BYTES),
    )(rows, *pieces)


def self_kernel(high_in, low_in, leaf_high_in, leaf_low_in, out, high, low, leaf_high, leaf_low, sems):
    core, _, _, z = position()
    mine = core * RING + z
    groups = ((10, 5), (6, 4), (0, 6))

    def moves():
        pairs = [(leaf_high_in, leaf_high), (leaf_low_in, leaf_low)]
        for first, count in groups:
            span = pl.ds(first, count)
            pairs += [(high_in.at[span], high.at[span]), (low_in.at[span], low.at[span])]
        return [pltpu.make_async_copy(a, b, sems.at[n]) for n, (a, b) in enumerate(pairs)]

    for move in moves():
        move.start()
    waiting = moves()
    waiting[0].wait()
    waiting[1].wait()
    pick = (
        lax.rem(mine, 4) * ROWS + lax.broadcasted_iota(jnp.int32, (ROWS, 4 * ROWS), 0)
        == lax.broadcasted_iota(jnp.int32, (ROWS, 4 * ROWS), 1)
    ).astype(jnp.bfloat16)
    sides = []
    for level in range(5):
        found = []
        for leaf in range(2):
            lane = pl.multiple_of(leaf * NW + mine // 4 * 4 * ROWS, 4 * ROWS)
            cut = pl.ds(lane, 4 * ROWS)
            found.append(
                product(pick, leaf_high[level, :, cut], True)
                + product(pick, leaf_low[level, :, cut], True)
            )
        sides.append(jnp.concatenate(found, axis=0))

    def ready(level):
        if level >= 2:
            waiting[2 + 2 * (4 - level)].wait()
            waiting[3 + 2 * (4 - level)].wait()

    _, pairs = sweep(sides, high, low, None, ready)
    for leaf in range(2):
        span = slice(leaf * NW, (leaf + 1) * NW)
        rows = slice(leaf * ROWS, (leaf + 1) * ROWS)
        total = None
        for level in range(5):
            pair = (pairs[level][0][rows], pairs[level][1][rows])
            term = triple(pair, leaf_high[level, :, span], leaf_low[level, :, span], False)
            total = term if total is None else total + term
        out[:, span] = total


def self_rows(high, low, leaf_high, leaf_low):
    return pl.pallas_call(
        self_kernel,
        out_shape=jax.ShapeDtypeStruct((ROWS, 2 * NW), jnp.float32),
        in_specs=[pl.BlockSpec(memory_space=pl.ANY)] * 4,
        out_specs=pl.BlockSpec(memory_space=pltpu.VMEM),
        scratch_shapes=[
            pltpu.VMEM((15, NW, NW), jnp.bfloat16),
            pltpu.VMEM((15, NW, NW), jnp.bfloat16),
            pltpu.VMEM((5, NW, 2 * NW), jnp.bfloat16),
            pltpu.VMEM((5, NW, 2 * NW), jnp.bfloat16),
            pltpu.SemaphoreType.DMA((8,)),
        ],
        compiler_params=pltpu.CompilerParams(vmem_limit_bytes=VMEM_BYTES),
    )(high, low, leaf_high, leaf_low)


def per_device(
    pattern,
    pivot_root,
    pivot_first,
    factor_first,
    pivot_second,
    factor_second,
    pivot_third,
    factor_third,
    pivot_fourth,
    factor_fourth,
    pivot_leaves,
    factor_leaves,
):
    sn = lax.axis_index("sn")
    core, x_low, y_lo, z = position()
    x_high = sn // 4 % 2
    y_high = sn // 8
    own = core == y_lo

    first, second, third, fourth, leaves = mask_all(
        pattern,
        (factor_first, factor_second, factor_third, factor_fourth, factor_leaves),
        (pivot_first, pivot_second, pivot_third, pivot_fourth),
    )

    fourth = jnp.where(own, fourth, send(fourth, TURN))
    fourth = ordered(fourth, send(fourth, CORE), core)
    leaves = jnp.where(own, leaves, send(leaves, TURN))
    leaves = ordered(leaves, send(leaves, CORE), core)

    third = join(third, CORE, core)
    second = join(second, CORE, core)
    first = join(first, CORE, core)
    root = join(pivot_root[None], CORE, core)
    first = join(first, X_LOW, x_low)
    root = join(root, X_LOW, x_low)
    first = join(first, X_HIGH, x_high)
    root = join(root, X_HIGH, x_high)
    root = join(root, Y_HIGH, y_high)
    low_two = lax.dynamic_slice_in_dim(jnp.concatenate([first, root], axis=0), x_low * W, W, 2)
    upper = jnp.concatenate(
        [jnp.stack([second, low_two]), jnp.stack([third[:, :, :W], third[:, :, W:]])], axis=1
    )

    steps, far = ring(upper, core)
    ends = jnp.stack([lax.dynamic_index_in_dim(upper, core, 0, keepdims=False), far])
    lower = jnp.stack([piece[:, :3] for piece in steps + [ends]])
    third = jnp.stack([piece[:, 3:] for piece in steps + [ends]])
    lower_y = send(lower, Y_LOW)
    lower_x = send(lower, X_LOW)
    third_y = send(third, Y_LOW)
    lower_yx = send(lower_y, X_LOW)
    lower_all = []
    for part in (lower, lower_x, lower_y, lower_yx):
        lower_all += [part, send(part, CORE)]
    third_all = []
    for part in (third, third_y):
        third_all += [part, send(part, CORE)]

    def collect(shard):
        steps, far = ring(shard, core)
        return [shard] + steps + [send(step, CORE) for step in steps] + [far, send(far, CORE)]

    rows, high, low = path_rows(collect(fourth), lower_all, third_all)
    pairs, leaf_high, leaf_low = pair_rows(rows, collect(leaves))
    pairs = jnp.where(own, pairs, send(pairs, TURN))
    selves = self_rows(high, low, leaf_high, leaf_low)
    selves = jnp.where(own, selves, send(selves, TURN))
    return pairs, pivot_leaves + selves


def solution(mesh):
    tree = P("pan", "sn")
    panel = P(None, "pan", "sn")
    return jax.shard_map(
        per_device,
        mesh=mesh,
        in_specs=(P(), tree, tree, panel, tree, panel, tree, panel, tree, panel, tree, panel),
        out_specs=(panel, tree),
        check_vma=False,
    )
```

```python
import jax
import jax.numpy as jnp
from jax import lax
from jax.experimental import pallas as pl
from jax.experimental.pallas import tpu as pltpu
from jax.sharding import PartitionSpec as P

W = 256
SUPERS = 2
NW = 512
ROWS = 32
RING = 8
FIRST_BLOCK = {1: 3, 2: 0, 3: 6, 4: 10}
PIVOT_BLOCK = {0: 5, 1: 4, 2: 2, 3: 9, 4: 14}
VMEM_BYTES = 52 * 1024 * 1024

def place(index):
    sn, pan = divmod(index, 16)
    y_hi, rest = divmod(sn, 8)
    x, core = divmod(rest, 2)
    y_lo, z = divmod(pan, RING)
    return y_hi, x, core, y_lo, z


def number(y_hi, x, core, y_lo, z):
    return (y_hi * 8 + x * 2 + core) * 16 + y_lo * RING + z


def route(move):
    pairs = []
    for index in range(256):
        target = number(*move(*place(index)))
        if target != index:
            pairs.append((index, target))
    return pairs


CORE = route(lambda yh, x, c, yl, z: (yh, x, 1 - c, yl, z))
X_LOW = route(lambda yh, x, c, yl, z: (yh, x ^ 1, c, yl, z))
X_HIGH = route(lambda yh, x, c, yl, z: (yh, x ^ 2, c, yl, z))
Y_HIGH = route(lambda yh, x, c, yl, z: (1 - yh, x, c, yl, z))
Y_LOW = route(lambda yh, x, c, yl, z: (yh, x, c, 1 - yl, z))
TURN = route(lambda yh, x, c, yl, z: (yh, x, yl, c, z))
Z_BOTH = route(lambda yh, x, c, yl, z: (yh, x, c, yl, (z + 1 - 2 * c) % RING))


def send(block, pairs):
    return lax.ppermute(block, ("sn", "pan"), pairs)


def join(block, pairs, bit):
    other = send(block, pairs)
    return jnp.where(
        bit == 1,
        jnp.concatenate([other, block], axis=-1),
        jnp.concatenate([block, other], axis=-1),
    )


def ring(shard, core):
    found = []
    held = shard
    for step in range(3):
        held = send(held, Z_BOTH)
        found.append(held)
    far = send(lax.dynamic_index_in_dim(held, core, 0, keepdims=False), Z_BOTH)
    return found, far


def ordered(mine, other, core):
    return jnp.where(core == 0, jnp.stack([mine, other]), jnp.stack([other, mine]))


def position():
    sn = lax.axis_index("sn")
    pan = lax.axis_index("pan")
    return sn % 2, sn // 2 % 2, pan // RING, pan % RING


def mask_kernel(pattern, *refs):
    sn = lax.axis_index("sn")
    y_lo = lax.axis_index("pan") // RING
    ins, outs = refs[:9], refs[9:]
    for level in range(1, 6):
        factor, out = ins[level - 1], outs[level - 1]
        cols = factor.shape[2]
        count = max(1, cols // W)
        width = cols // count
        for above in range(level):
            for part in range(count):
                scale = pattern[level, above * SUPERS + y_lo, sn * cols // W + part]
                span = slice(part * width, (part + 1) * width)
                out[above, :, span] = factor[above, :, span] * scale.astype(jnp.float32)
        if level < 5:
            out[level] = ins[4 + level][...]


def mask_all(pattern, factors, pivots):
    shapes = [
        jax.ShapeDtypeStruct((f.shape[0] + (f.shape[0] < 5),) + f.shape[1:], jnp.float32)
        for f in factors
    ]
    vmem = pl.BlockSpec(memory_space=pltpu.VMEM)
    return pl.pallas_call(
        mask_kernel,
        out_shape=shapes,
        in_specs=[pl.BlockSpec(memory_space=pltpu.SMEM)] + [vmem] * 9,
        out_specs=[vmem] * 5,
    )(pattern, *factors, *pivots)


def split(value):
    high = value.astype(jnp.bfloat16)
    return high, (value - high.astype(jnp.float32)).astype(jnp.bfloat16)


def product(left, right, turned):
    dims = (((1,), (1 if turned else 0,)), ((), ()))
    return lax.dot_general(left, right, dims, preferred_element_type=jnp.float32)


def triple(pair, high, low, turned):
    rows = pair[0].shape[0]
    both = product(jnp.concatenate(pair, axis=0), high, turned)
    return both[:rows] + both[rows:] + product(pair[0], low, turned)


def sweep(parts, high, low, unit, ready):
    parts = list(parts)
    for level in range(4, -1, -1):
        if unit is not None:
            known = [] if parts[level] is None else [parts[level]]
            parts[level] = jnp.concatenate(known + [unit], axis=0)
        if level == 0:
            break
        ready(level)
        pair = split(parts[level])
        for above in range(level):
            block = FIRST_BLOCK[level] + above
            piece = triple(pair, high[block], low[block], True)
            if parts[above] is None:
                parts[above] = -piece
            else:
                held = parts[above].shape[0]
                if held == piece.shape[0]:
                    parts[above] = parts[above] - piece
                else:
                    parts[above] = jnp.concatenate([parts[above] - piece[:held], -piece[held:]], 0)
    ready(0)
    done = [
        triple(split(part), high[PIVOT_BLOCK[level]], low[PIVOT_BLOCK[level]], False)
        for level, part in enumerate(parts)
    ]
    pairs = [split(done[0])]
    for level in range(1, 5):
        total = None
        for above in range(level):
            block = FIRST_BLOCK[level] + above
            term = triple(pairs[above], high[block], low[block], False)
            total = term if total is None else total + term
        held = done[level].shape[0]
        if held == total.shape[0]:
            done[level] = done[level] - total
        else:
            done[level] = jnp.concatenate([done[level] - total[:held], -total[held:]], axis=0)
        pairs.append(split(done[level]))
    return done, pairs


def whole_wait(ref, sem):
    pltpu.make_async_copy(ref, ref, sem).wait()


def path_kernel(*refs):
    (fourth_own, f1, f2, f3, g1, g2, g3, f_far, g_far), refs = refs[:9], refs[9:]
    third, second, lowest = refs[:4], refs[4:12], refs[12:20]
    rows_out, high_out, low_out = refs[20:23]
    raw, high, low, in_sem, out_sem = refs[23:]
    core, x_low, y_lo, z = position()
    mine = core * RING + z
    far_z = lax.rem(z + 4, RING)

    def turn(step, own):
        sign = 2 * core - 1 if own else 1 - 2 * core
        return lax.rem(z + sign * step + RING, RING)

    def side(own):
        return core if own else 1 - core

    def copy(source, first, row, lane, sem):
        count, rows, width = source.shape
        row = pl.multiple_of(row, rows)
        if not isinstance(lane, int):
            lane = pl.multiple_of(lane, W)
        pltpu.make_async_copy(
            source, raw.at[pl.ds(first, count), pl.ds(row, rows), pl.ds(lane, width)], in_sem.at[sem]
        ).start()

    for half in range(2):
        copy(fourth_own.at[half], 10, (half * RING + z) * ROWS, 0, 0)
        for step, (a, b) in enumerate(((f1, g1), (f2, g2), (f3, g3)), 1):
            copy(a.at[half], 10, (half * RING + turn(step, True)) * ROWS, 0, 0)
            copy(b.at[half], 10, (half * RING + turn(step, False)) * ROWS, 0, 0)
    copy(f_far, 10, (side(True) * RING + far_z) * ROWS, 0, 0)
    copy(g_far, 10, (side(False) * RING + far_z) * ROWS, 0, 0)

    def spread(source, own, base, first, lane, sem):
        for step in range(3):
            for half in range(2):
                row = (base + turn(step + 1, own)) * ROWS + half * (ROWS // 2)
                copy(source.at[step, half], first, row, lane, sem)
        for end, place_z in enumerate((z, far_z)):
            row = (base + place_z) * ROWS + side(own) * (ROWS // 2)
            copy(source.at[3, end], first, row, lane, sem)

    for index, source in enumerate(third):
        base = (y_lo if index // 2 == 0 else 1 - y_lo) * RING
        for part in range(2):
            spread(source.at[:, :, pl.ds(part * 4, 4)], index % 2 == 0, base, 6, part * W, 1)
    for first, sources in ((0, second), (3, lowest)):
        for index, source in enumerate(sources):
            base = (y_lo if index // 4 == 0 else 1 - y_lo) * RING
            lane = (x_low if index // 2 % 2 == 0 else 1 - x_low) * W
            spread(source, index % 2 == 0, base, first, lane, 2)

    def take(first, count, sem):
        whole_wait(raw.at[pl.ds(first, count)], in_sem.at[sem])

        for block in range(first, first + count):
            high[block], low[block] = split(raw[block])
        span = pl.ds(first, count)
        pltpu.make_async_copy(high.at[span], high_out.at[span], out_sem.at[2 * sem]).start()
        pltpu.make_async_copy(low.at[span], low_out.at[span], out_sem.at[2 * sem + 1]).start()

    def ready(level):
        if level == 4:
            take(10, 5, 0)
        if level == 3:
            take(6, 4, 1)
        if level == 2:
            take(0, 6, 2)

    unit = (
        mine * ROWS + lax.broadcasted_iota(jnp.int32, (ROWS, NW), 0)
        == lax.broadcasted_iota(jnp.int32, (ROWS, NW), 1)
    ).astype(jnp.float32)
    done, _ = sweep([None] * 5, high, low, unit, ready)
    for level in range(5):
        rows_out[:, level * NW : (level + 1) * NW] = done[level]
    for sem, (first, count) in enumerate(((10, 5), (6, 4), (0, 6))):
        span = pl.ds(first, count)
        pltpu.make_async_copy(high.at[span], high_out.at[span], out_sem.at[2 * sem]).wait()
        pltpu.make_async_copy(low.at[span], low_out.at[span], out_sem.at[2 * sem + 1]).wait()


def path_rows(*pieces):
    held = jax.ShapeDtypeStruct((15, NW, NW), jnp.bfloat16)
    return pl.pallas_call(
        path_kernel,
        out_shape=[jax.ShapeDtypeStruct((5 * ROWS, 5 * NW), jnp.float32), held, held],
        in_specs=[pl.BlockSpec(memory_space=pl.ANY)] * len(pieces),
        out_specs=[
            pl.BlockSpec(memory_space=pltpu.VMEM),
            pl.BlockSpec(memory_space=pl.ANY),
            pl.BlockSpec(memory_space=pl.ANY),
        ],
        scratch_shapes=[
            pltpu.VMEM((15, NW, NW), jnp.float32),
            pltpu.VMEM((15, NW, NW), jnp.bfloat16),
            pltpu.VMEM((15, NW, NW), jnp.bfloat16),
            pltpu.SemaphoreType.DMA((3,)),
            pltpu.SemaphoreType.DMA((6,)),
        ],
        cost_estimate=pl.CostEstimate(flops=10**10, bytes_accessed=32 * 10**6, transcendentals=0),
        compiler_params=pltpu.CompilerParams(vmem_limit_bytes=VMEM_BYTES),
    )(*pieces)


def pair_kernel(rows, own_shard, f1, f2, f3, g1, g2, g3, f_far, g_far, out, sides_out, high_out, low_out, raw, high, low, in_sem, out_sem):
    core, _, _, z = position()
    far_z = lax.rem(z + 4, RING)

    def turn(step, own):
        sign = 2 * core - 1 if own else 1 - 2 * core
        return lax.rem(z + sign * step + RING, RING)

    for level in range(5):

        def copy(source, row):
            row = pl.multiple_of(row * ROWS, ROWS)
            pltpu.make_async_copy(source, raw.at[level, pl.ds(row, ROWS)], in_sem.at[level]).start()

        for half in range(2):
            copy(own_shard.at[half, level], half * RING + z)
            for step, (a, b) in enumerate(((f1, g1), (f2, g2), (f3, g3)), 1):
                copy(a.at[half, level], half * RING + turn(step, True))
                copy(b.at[half, level], half * RING + turn(step, False))
        copy(f_far.at[level], core * RING + far_z)
        copy(g_far.at[level], (1 - core) * RING + far_z)

    total = None
    for level in range(5):
        whole_wait(raw.at[level], in_sem.at[level])
        for part in range(2):
            span = slice(part * NW, (part + 1) * NW)
            high[level, :, span], low[level, :, span] = split(raw[level, :, span])
        pltpu.make_async_copy(high.at[level], high_out.at[level], out_sem.at[level, 0]).start()
        pltpu.make_async_copy(low.at[level], low_out.at[level], out_sem.at[level, 1]).start()
        pair = split(rows[:, level * NW : (level + 1) * NW])
        term = triple(pair, high[level], low[level], False)
        total = term if total is None else total + term
    for level in range(5):
        first = (4 - level) * ROWS
        out[level] = -total[first : first + ROWS]
    mine = core * RING + z
    pick = (
        lax.rem(mine, 4) * ROWS + lax.broadcasted_iota(jnp.int32, (ROWS, 4 * ROWS), 0)
        == lax.broadcasted_iota(jnp.int32, (ROWS, 4 * ROWS), 1)
    ).astype(jnp.bfloat16)
    for level in range(5):
        for leaf in range(2):
            lane = pl.multiple_of(leaf * NW + mine // 4 * 4 * ROWS, 4 * ROWS)
            cut = pl.ds(lane, 4 * ROWS)
            sides_out[level, leaf * ROWS : (leaf + 1) * ROWS] = product(
                pick, high[level, :, cut], True
            ) + product(pick, low[level, :, cut], True)
    for level in range(5):
        pltpu.make_async_copy(high.at[level], high_out.at[level], out_sem.at[level, 0]).wait()
        pltpu.make_async_copy(low.at[level], low_out.at[level], out_sem.at[level, 1]).wait()


def pair_rows(rows, pieces):
    held = jax.ShapeDtypeStruct((5, NW, 2 * NW), jnp.bfloat16)
    return pl.pallas_call(
        pair_kernel,
        out_shape=[
            jax.ShapeDtypeStruct((5, ROWS, 2 * NW), jnp.float32),
            jax.ShapeDtypeStruct((5, 2 * ROWS, NW), jnp.float32),
            held,
            held,
        ],
        in_specs=[pl.BlockSpec(memory_space=pltpu.VMEM)] + [pl.BlockSpec(memory_space=pl.ANY)] * 9,
        out_specs=[
            pl.BlockSpec(memory_space=pltpu.VMEM),
            pl.BlockSpec(memory_space=pltpu.VMEM),
            pl.BlockSpec(memory_space=pl.ANY),
            pl.BlockSpec(memory_space=pl.ANY),
        ],
        scratch_shapes=[
            pltpu.VMEM((5, NW, 2 * NW), jnp.float32),
            pltpu.VMEM((5, NW, 2 * NW), jnp.bfloat16),
            pltpu.VMEM((5, NW, 2 * NW), jnp.bfloat16),
            pltpu.SemaphoreType.DMA((5,)),
            pltpu.SemaphoreType.DMA((5, 2)),
        ],
        cost_estimate=pl.CostEstimate(flops=5 * 10**9, bytes_accessed=21 * 10**6, transcendentals=0),
        compiler_params=pltpu.CompilerParams(vmem_limit_bytes=VMEM_BYTES),
    )(rows, *pieces)


def self_kernel(sides, high_in, low_in, leaf_high_in, leaf_low_in, out, high, low, leaf_high, leaf_low, sems):
    def moves():
        pairs = []
        for first, count in ((10, 5), (6, 4), (0, 6)):
            span = pl.ds(first, count)
            pairs += [(high_in.at[span], high.at[span]), (low_in.at[span], low.at[span])]
        pairs += [(leaf_high_in, leaf_high), (leaf_low_in, leaf_low)]
        return [pltpu.make_async_copy(a, b, sems.at[n]) for n, (a, b) in enumerate(pairs)]

    for move in moves():
        move.start()
    waiting = moves()

    def ready(level):
        if level >= 2:
            waiting[2 * (4 - level)].wait()
            waiting[2 * (4 - level) + 1].wait()

    _, pairs = sweep([sides[level] for level in range(5)], high, low, None, ready)
    waiting[6].wait()
    waiting[7].wait()
    for leaf in range(2):
        span = slice(leaf * NW, (leaf + 1) * NW)
        rows = slice(leaf * ROWS, (leaf + 1) * ROWS)
        total = None
        for level in range(5):
            pair = (pairs[level][0][rows], pairs[level][1][rows])
            term = triple(pair, leaf_high[level, :, span], leaf_low[level, :, span], False)
            total = term if total is None else total + term
        out[:, span] = total


def self_rows(sides, high, low, leaf_high, leaf_low):
    return pl.pallas_call(
        self_kernel,
        out_shape=jax.ShapeDtypeStruct((ROWS, 2 * NW), jnp.float32),
        in_specs=[pl.BlockSpec(memory_space=pltpu.VMEM)] + [pl.BlockSpec(memory_space=pl.ANY)] * 4,
        out_specs=pl.BlockSpec(memory_space=pltpu.VMEM),
        scratch_shapes=[
            pltpu.VMEM((15, NW, NW), jnp.bfloat16),
            pltpu.VMEM((15, NW, NW), jnp.bfloat16),
            pltpu.VMEM((5, NW, 2 * NW), jnp.bfloat16),
            pltpu.VMEM((5, NW, 2 * NW), jnp.bfloat16),
            pltpu.SemaphoreType.DMA((8,)),
        ],
        cost_estimate=pl.CostEstimate(flops=5 * 10**9, bytes_accessed=26 * 10**6, transcendentals=0),
        compiler_params=pltpu.CompilerParams(vmem_limit_bytes=VMEM_BYTES),
    )(sides, high, low, leaf_high, leaf_low)


def per_device(
    pattern,
    pivot_root,
    pivot_first,
    factor_first,
    pivot_second,
    factor_second,
    pivot_third,
    factor_third,
    pivot_fourth,
    factor_fourth,
    pivot_leaves,
    factor_leaves,
):
    sn = lax.axis_index("sn")
    core, x_low, y_lo, z = position()
    x_high = sn // 4 % 2
    y_high = sn // 8
    own = core == y_lo

    first, second, third, fourth, leaves = mask_all(
        pattern,
        (factor_first, factor_second, factor_third, factor_fourth, factor_leaves),
        (pivot_first, pivot_second, pivot_third, pivot_fourth),
    )

    def halves(blocks):
        count, rows, width = blocks.shape
        return blocks.reshape(count, 2, rows // 2, width).transpose(1, 0, 2, 3)

    def collect(shard):
        steps, far = ring(shard, core)
        return [shard] + steps + [send(step, CORE) for step in steps] + [far, send(far, CORE)]

    def gathered(shard):
        steps, far = ring(shard, core)
        ends = jnp.stack([lax.dynamic_index_in_dim(shard, core, 0, keepdims=False), far])
        return steps + [ends]

    def both(pack):
        return [pack, send(pack, CORE)]

    def four(pack):
        pack_y = send(pack, Y_LOW)
        pack_x = send(pack, X_LOW)
        pack_yx = send(pack_y, X_LOW)
        return both(pack) + both(pack_x) + both(pack_y) + both(pack_yx)

    third = join(third, CORE, core)
    second = join(second, CORE, core)
    upper = halves(jnp.concatenate([third[:, :, :W], third[:, :, W:], second], axis=0))
    upper = gathered(upper)
    second = jnp.stack([piece[:, 8:] for piece in upper])
    third = jnp.stack([piece[:, :8] for piece in upper])
    second_all = four(second)
    third_all = both(third) + both(send(third, Y_LOW))

    fourth = jnp.where(own, fourth, send(fourth, TURN))
    fourth = ordered(fourth, send(fourth, CORE), core)
    fourth_all = collect(fourth)
    leaves = jnp.where(own, leaves, send(leaves, TURN))
    leaves = ordered(leaves, send(leaves, CORE), core)
    leaves_all = collect(leaves)

    first = join(first, CORE, core)
    root = join(pivot_root[None], CORE, core)
    first = join(first, X_LOW, x_low)
    root = join(root, X_LOW, x_low)
    first = join(first, X_HIGH, x_high)
    root = join(root, X_HIGH, x_high)
    root = join(root, Y_HIGH, y_high)
    lowest = lax.dynamic_slice_in_dim(jnp.concatenate([first, root], axis=0), x_low * W, W, 2)
    lowest_all = four(jnp.stack(gathered(halves(lowest))))

    rows, high, low = path_rows(*fourth_all, *third_all, *second_all, *lowest_all)
    pairs, sides, leaf_high, leaf_low = pair_rows(rows, leaves_all)
    pairs = jnp.where(own, pairs, send(pairs, TURN))
    selves = self_rows(sides, high, low, leaf_high, leaf_low)
    selves = jnp.where(own, selves, send(selves, TURN))
    return pairs, pivot_leaves + selves


def solution(mesh):
    tree = P("pan", "sn")
    panel = P(None, "pan", "sn")
    return jax.shard_map(
        per_device,
        mesh=mesh,
        in_specs=(P(), tree, tree, panel, tree, panel, tree, panel, tree, panel, tree, panel),
        out_specs=(panel, tree),
        check_vma=False,
    )
```

```python
import jax
import jax.numpy as jnp
from jax import lax
from jax.experimental import pallas as pl
from jax.experimental.pallas import tpu as pltpu
from jax.sharding import PartitionSpec as P

W = 256
SUPERS = 2
NW = 512
ROWS = 32
RING = 8
FIRST_BLOCK = {1: 3, 2: 0, 3: 6, 4: 10}
PIVOT_BLOCK = {0: 5, 1: 4, 2: 2, 3: 9, 4: 14}
VMEM_BYTES = 52 * 1024 * 1024

def place(index):
    sn, pan = divmod(index, 16)
    y_hi, rest = divmod(sn, 8)
    x, core = divmod(rest, 2)
    y_lo, z = divmod(pan, RING)
    return y_hi, x, core, y_lo, z


def number(y_hi, x, core, y_lo, z):
    return (y_hi * 8 + x * 2 + core) * 16 + y_lo * RING + z


def route(move):
    pairs = []
    for index in range(256):
        target = number(*move(*place(index)))
        if target != index:
            pairs.append((index, target))
    return pairs


CORE = route(lambda yh, x, c, yl, z: (yh, x, 1 - c, yl, z))
X_LOW = route(lambda yh, x, c, yl, z: (yh, x ^ 1, c, yl, z))
X_HIGH = route(lambda yh, x, c, yl, z: (yh, x ^ 2, c, yl, z))
Y_HIGH = route(lambda yh, x, c, yl, z: (1 - yh, x, c, yl, z))
Y_LOW = route(lambda yh, x, c, yl, z: (yh, x, c, 1 - yl, z))
TURN = route(lambda yh, x, c, yl, z: (yh, x, yl, c, z))
Z_BOTH = route(lambda yh, x, c, yl, z: (yh, x, c, yl, (z + 1 - 2 * c) % RING))


def send(block, pairs):
    return lax.ppermute(block, ("sn", "pan"), pairs)


def join(block, pairs, bit):
    other = send(block, pairs)
    return jnp.where(
        bit == 1,
        jnp.concatenate([other, block], axis=-1),
        jnp.concatenate([block, other], axis=-1),
    )


def ring(shard, core):
    found = []
    held = shard
    for step in range(3):
        held = send(held, Z_BOTH)
        found.append(held)
    far = send(lax.dynamic_index_in_dim(held, core, 0, keepdims=False), Z_BOTH)
    return found, far


def ordered(mine, other, core):
    return jnp.where(core == 0, jnp.stack([mine, other]), jnp.stack([other, mine]))


def position():
    sn = lax.axis_index("sn")
    pan = lax.axis_index("pan")
    return sn % 2, sn // 2 % 2, pan // RING, pan % RING


def mask_kernel(pattern, *refs):
    sn = lax.axis_index("sn")
    y_lo = lax.axis_index("pan") // RING
    ins, outs = refs[:9], refs[9:]
    for level in range(1, 6):
        factor, out = ins[level - 1], outs[level - 1]
        cols = factor.shape[2]
        count = max(1, cols // W)
        width = cols // count
        for above in range(level):
            for part in range(count):
                scale = pattern[level, above * SUPERS + y_lo, sn * cols // W + part]
                span = slice(part * width, (part + 1) * width)
                out[above, :, span] = factor[above, :, span] * scale.astype(jnp.float32)
        if level < 5:
            out[level] = ins[4 + level][...]


def mask_all(pattern, factors, pivots):
    shapes = [
        jax.ShapeDtypeStruct((f.shape[0] + (f.shape[0] < 5),) + f.shape[1:], jnp.float32)
        for f in factors
    ]
    vmem = pl.BlockSpec(memory_space=pltpu.VMEM)
    return pl.pallas_call(
        mask_kernel,
        out_shape=shapes,
        in_specs=[pl.BlockSpec(memory_space=pltpu.SMEM)] + [vmem] * 9,
        out_specs=[vmem] * 5,
    )(pattern, *factors, *pivots)


def split(value):
    high = value.astype(jnp.bfloat16)
    return high, (value - high.astype(jnp.float32)).astype(jnp.bfloat16)


def product(left, right, turned):
    dims = (((1,), (1 if turned else 0,)), ((), ()))
    return lax.dot_general(left, right, dims, preferred_element_type=jnp.float32)


def triple(pair, high, low, turned):
    rows = pair[0].shape[0]
    both = product(jnp.concatenate(pair, axis=0), high, turned)
    return both[:rows] + both[rows:] + product(pair[0], low, turned)


def sweep(parts, high, low, unit, ready):
    parts = list(parts)
    for level in range(4, -1, -1):
        if unit is not None:
            known = [] if parts[level] is None else [parts[level]]
            parts[level] = jnp.concatenate(known + [unit], axis=0)
        if level == 0:
            break
        ready(level)
        pair = split(parts[level])
        for above in range(level):
            block = FIRST_BLOCK[level] + above
            piece = triple(pair, high[block], low[block], True)
            if parts[above] is None:
                parts[above] = -piece
            else:
                held = parts[above].shape[0]
                if held == piece.shape[0]:
                    parts[above] = parts[above] - piece
                else:
                    parts[above] = jnp.concatenate([parts[above] - piece[:held], -piece[held:]], 0)
    ready(0)
    done = [
        triple(split(part), high[PIVOT_BLOCK[level]], low[PIVOT_BLOCK[level]], False)
        for level, part in enumerate(parts)
    ]
    pairs = [split(done[0])]
    for level in range(1, 5):
        total = None
        for above in range(level):
            block = FIRST_BLOCK[level] + above
            term = triple(pairs[above], high[block], low[block], False)
            total = term if total is None else total + term
        held = done[level].shape[0]
        if held == total.shape[0]:
            done[level] = done[level] - total
        else:
            done[level] = jnp.concatenate([done[level] - total[:held], -total[held:]], axis=0)
        pairs.append(split(done[level]))
    return done, pairs


def whole_wait(ref, sem):
    pltpu.make_async_copy(ref, ref, sem).wait()


def path_kernel(*refs):
    (fourth_own, f1, f2, f3, g1, g2, g3, f_far, g_far), refs = refs[:9], refs[9:]
    third, second, lowest = refs[:4], refs[4:12], refs[12:20]
    rows_out, high_out, low_out = refs[20:23]
    raw, high, low, in_sem, out_sem = refs[23:]
    core, x_low, y_lo, z = position()
    mine = core * RING + z
    far_z = lax.rem(z + 4, RING)

    def turn(step, own):
        sign = 2 * core - 1 if own else 1 - 2 * core
        return lax.rem(z + sign * step + RING, RING)

    def side(own):
        return core if own else 1 - core

    def copy(source, first, row, lane, sem):
        count, rows, width = source.shape
        row = pl.multiple_of(row, rows)
        if not isinstance(lane, int):
            lane = pl.multiple_of(lane, W)
        pltpu.make_async_copy(
            source, raw.at[pl.ds(first, count), pl.ds(row, rows), pl.ds(lane, width)], in_sem.at[sem]
        ).start()

    for half in range(2):
        copy(fourth_own.at[half], 10, (half * RING + z) * ROWS, 0, 0)
        for step, (a, b) in enumerate(((f1, g1), (f2, g2), (f3, g3)), 1):
            copy(a.at[half], 10, (half * RING + turn(step, True)) * ROWS, 0, 0)
            copy(b.at[half], 10, (half * RING + turn(step, False)) * ROWS, 0, 0)
    copy(f_far, 10, (side(True) * RING + far_z) * ROWS, 0, 0)
    copy(g_far, 10, (side(False) * RING + far_z) * ROWS, 0, 0)

    def spread(source, own, base, first, lane, sem):
        for step in range(3):
            for half in range(2):
                row = (base + turn(step + 1, own)) * ROWS + half * (ROWS // 2)
                copy(source.at[step, half], first, row, lane, sem)
        for end, place_z in enumerate((z, far_z)):
            row = (base + place_z) * ROWS + side(own) * (ROWS // 2)
            copy(source.at[3, end], first, row, lane, sem)

    for index, source in enumerate(third):
        base = (y_lo if index // 2 == 0 else 1 - y_lo) * RING
        for part in range(2):
            spread(source.at[:, :, pl.ds(part * 4, 4)], index % 2 == 0, base, 6, part * W, 1)
    for first, sources in ((0, second), (3, lowest)):
        for index, source in enumerate(sources):
            base = (y_lo if index // 4 == 0 else 1 - y_lo) * RING
            lane = (x_low if index // 2 % 2 == 0 else 1 - x_low) * W
            spread(source, index % 2 == 0, base, first, lane, 2)

    def take(first, count, sem):
        whole_wait(raw.at[pl.ds(first, count)], in_sem.at[sem])

        for block in range(first, first + count):
            high[block], low[block] = split(raw[block])
        span = pl.ds(first, count)
        pltpu.make_async_copy(high.at[span], high_out.at[span], out_sem.at[2 * sem]).start()
        pltpu.make_async_copy(low.at[span], low_out.at[span], out_sem.at[2 * sem + 1]).start()

    def ready(level):
        if level == 4:
            take(10, 5, 0)
        if level == 3:
            take(6, 4, 1)
        if level == 2:
            take(0, 6, 2)

    unit = (
        mine * ROWS + lax.broadcasted_iota(jnp.int32, (ROWS, NW), 0)
        == lax.broadcasted_iota(jnp.int32, (ROWS, NW), 1)
    ).astype(jnp.float32)
    done, _ = sweep([None] * 5, high, low, unit, ready)
    for level in range(5):
        rows_out[:, level * NW : (level + 1) * NW] = done[level]
    for sem, (first, count) in enumerate(((10, 5), (6, 4), (0, 6))):
        span = pl.ds(first, count)
        pltpu.make_async_copy(high.at[span], high_out.at[span], out_sem.at[2 * sem]).wait()
        pltpu.make_async_copy(low.at[span], low_out.at[span], out_sem.at[2 * sem + 1]).wait()


def path_rows(*pieces):
    held = jax.ShapeDtypeStruct((15, NW, NW), jnp.bfloat16)
    return pl.pallas_call(
        path_kernel,
        out_shape=[jax.ShapeDtypeStruct((5 * ROWS, 5 * NW), jnp.float32), held, held],
        in_specs=[pl.BlockSpec(memory_space=pl.ANY)] * len(pieces),
        out_specs=[
            pl.BlockSpec(memory_space=pltpu.VMEM),
            pl.BlockSpec(memory_space=pl.ANY),
            pl.BlockSpec(memory_space=pl.ANY),
        ],
        scratch_shapes=[
            pltpu.VMEM((15, NW, NW), jnp.float32),
            pltpu.VMEM((15, NW, NW), jnp.bfloat16),
            pltpu.VMEM((15, NW, NW), jnp.bfloat16),
            pltpu.SemaphoreType.DMA((3,)),
            pltpu.SemaphoreType.DMA((6,)),
        ],
        cost_estimate=pl.CostEstimate(flops=10**10, bytes_accessed=32 * 10**6, transcendentals=0),
        compiler_params=pltpu.CompilerParams(vmem_limit_bytes=VMEM_BYTES),
    )(*pieces)


def pair_kernel(rows, own_shard, f1, f2, f3, g1, g2, g3, f_far, g_far, out, sides_out, high_out, low_out, raw, high, low, in_sem, out_sem):
    core, _, _, z = position()
    far_z = lax.rem(z + 4, RING)

    def turn(step, own):
        sign = 2 * core - 1 if own else 1 - 2 * core
        return lax.rem(z + sign * step + RING, RING)

    for level in range(5):

        def copy(source, row):
            row = pl.multiple_of(row * ROWS, ROWS)
            pltpu.make_async_copy(source, raw.at[level, pl.ds(row, ROWS)], in_sem.at[level]).start()

        for half in range(2):
            copy(own_shard.at[half, level], half * RING + z)
            for step, (a, b) in enumerate(((f1, g1), (f2, g2), (f3, g3)), 1):
                copy(a.at[half, level], half * RING + turn(step, True))
                copy(b.at[half, level], half * RING + turn(step, False))
        copy(f_far.at[level], core * RING + far_z)
        copy(g_far.at[level], (1 - core) * RING + far_z)

    total = None
    for level in range(5):
        whole_wait(raw.at[level], in_sem.at[level])
        for part in range(2):
            span = slice(part * NW, (part + 1) * NW)
            high[level, :, span], low[level, :, span] = split(raw[level, :, span])
        pltpu.make_async_copy(high.at[level], high_out.at[level], out_sem.at[level, 0]).start()
        pltpu.make_async_copy(low.at[level], low_out.at[level], out_sem.at[level, 1]).start()
        pair = split(rows[:, level * NW : (level + 1) * NW])
        term = triple(pair, high[level], low[level], False)
        total = term if total is None else total + term
    for level in range(5):
        first = (4 - level) * ROWS
        out[level] = -total[first : first + ROWS]
    mine = core * RING + z
    pick = (
        lax.rem(mine, 4) * ROWS + lax.broadcasted_iota(jnp.int32, (ROWS, 4 * ROWS), 0)
        == lax.broadcasted_iota(jnp.int32, (ROWS, 4 * ROWS), 1)
    ).astype(jnp.bfloat16)
    for level in range(5):
        for leaf in range(2):
            lane = pl.multiple_of(leaf * NW + mine // 4 * 4 * ROWS, 4 * ROWS)
            cut = pl.ds(lane, 4 * ROWS)
            sides_out[level, leaf * ROWS : (leaf + 1) * ROWS] = product(
                pick, high[level, :, cut], True
            ) + product(pick, low[level, :, cut], True)
    for level in range(5):
        pltpu.make_async_copy(high.at[level], high_out.at[level], out_sem.at[level, 0]).wait()
        pltpu.make_async_copy(low.at[level], low_out.at[level], out_sem.at[level, 1]).wait()


def pair_rows(rows, pieces):
    held = jax.ShapeDtypeStruct((5, NW, 2 * NW), jnp.bfloat16)
    return pl.pallas_call(
        pair_kernel,
        out_shape=[
            jax.ShapeDtypeStruct((5, ROWS, 2 * NW), jnp.float32),
            jax.ShapeDtypeStruct((5, 2 * ROWS, NW), jnp.float32),
            held,
            held,
        ],
        in_specs=[pl.BlockSpec(memory_space=pltpu.VMEM)] + [pl.BlockSpec(memory_space=pl.ANY)] * 9,
        out_specs=[
            pl.BlockSpec(memory_space=pltpu.VMEM),
            pl.BlockSpec(memory_space=pltpu.VMEM),
            pl.BlockSpec(memory_space=pl.ANY),
            pl.BlockSpec(memory_space=pl.ANY),
        ],
        scratch_shapes=[
            pltpu.VMEM((5, NW, 2 * NW), jnp.float32),
            pltpu.VMEM((5, NW, 2 * NW), jnp.bfloat16),
            pltpu.VMEM((5, NW, 2 * NW), jnp.bfloat16),
            pltpu.SemaphoreType.DMA((5,)),
            pltpu.SemaphoreType.DMA((5, 2)),
        ],
        cost_estimate=pl.CostEstimate(flops=5 * 10**9, bytes_accessed=21 * 10**6, transcendentals=0),
        compiler_params=pltpu.CompilerParams(vmem_limit_bytes=VMEM_BYTES),
    )(rows, *pieces)


def self_kernel(sides, high_in, low_in, leaf_high_in, leaf_low_in, out, high, low, leaf_high, leaf_low, sems):
    def moves():
        pairs = []
        for first, count in ((10, 5), (6, 4), (0, 6)):
            span = pl.ds(first, count)
            pairs += [(high_in.at[span], high.at[span]), (low_in.at[span], low.at[span])]
        pairs += [(leaf_high_in, leaf_high), (leaf_low_in, leaf_low)]
        return [pltpu.make_async_copy(a, b, sems.at[n]) for n, (a, b) in enumerate(pairs)]

    for move in moves():
        move.start()
    waiting = moves()

    def ready(level):
        if level >= 2:
            waiting[2 * (4 - level)].wait()
            waiting[2 * (4 - level) + 1].wait()

    _, pairs = sweep([sides[level] for level in range(5)], high, low, None, ready)
    waiting[6].wait()
    waiting[7].wait()
    for leaf in range(2):
        span = slice(leaf * NW, (leaf + 1) * NW)
        rows = slice(leaf * ROWS, (leaf + 1) * ROWS)
        total = None
        for level in range(5):
            pair = (pairs[level][0][rows], pairs[level][1][rows])
            term = triple(pair, leaf_high[level, :, span], leaf_low[level, :, span], False)
            total = term if total is None else total + term
        out[:, span] = total


def self_rows(sides, high, low, leaf_high, leaf_low):
    return pl.pallas_call(
        self_kernel,
        out_shape=jax.ShapeDtypeStruct((ROWS, 2 * NW), jnp.float32),
        in_specs=[pl.BlockSpec(memory_space=pltpu.VMEM)] + [pl.BlockSpec(memory_space=pl.ANY)] * 4,
        out_specs=pl.BlockSpec(memory_space=pltpu.VMEM),
        scratch_shapes=[
            pltpu.VMEM((15, NW, NW), jnp.bfloat16),
            pltpu.VMEM((15, NW, NW), jnp.bfloat16),
            pltpu.VMEM((5, NW, 2 * NW), jnp.bfloat16),
            pltpu.VMEM((5, NW, 2 * NW), jnp.bfloat16),
            pltpu.SemaphoreType.DMA((8,)),
        ],
        cost_estimate=pl.CostEstimate(flops=5 * 10**9, bytes_accessed=26 * 10**6, transcendentals=0),
        compiler_params=pltpu.CompilerParams(vmem_limit_bytes=VMEM_BYTES),
    )(sides, high, low, leaf_high, leaf_low)


def per_device(
    pattern,
    pivot_root,
    pivot_first,
    factor_first,
    pivot_second,
    factor_second,
    pivot_third,
    factor_third,
    pivot_fourth,
    factor_fourth,
    pivot_leaves,
    factor_leaves,
):
    sn = lax.axis_index("sn")
    core, x_low, y_lo, z = position()
    x_high = sn // 4 % 2
    y_high = sn // 8
    own = core == y_lo

    first, second, third, fourth, leaves = mask_all(
        pattern,
        (factor_first, factor_second, factor_third, factor_fourth, factor_leaves),
        (pivot_first, pivot_second, pivot_third, pivot_fourth),
    )

    def halves(blocks):
        count, rows, width = blocks.shape
        return blocks.reshape(count, 2, rows // 2, width).transpose(1, 0, 2, 3)

    def collect(shard):
        steps, far = ring(shard, core)
        return [shard] + steps + [send(step, CORE) for step in steps] + [far, send(far, CORE)]

    def gathered(shard):
        steps, far = ring(shard, core)
        ends = jnp.stack([lax.dynamic_index_in_dim(shard, core, 0, keepdims=False), far])
        return steps + [ends]

    def both(pack):
        return [pack, send(pack, CORE)]

    def four(pack):
        pack_y = send(pack, Y_LOW)
        pack_x = send(pack, X_LOW)
        pack_yx = send(pack_y, X_LOW)
        return both(pack) + both(pack_x) + both(pack_y) + both(pack_yx)

    third = join(third, CORE, core)
    second = join(second, CORE, core)
    upper = halves(jnp.concatenate([third[:, :, :W], third[:, :, W:], second], axis=0))
    upper = gathered(upper)
    second = jnp.stack([piece[:, 8:] for piece in upper])
    third = jnp.stack([piece[:, :8] for piece in upper])
    second_all = four(second)
    third_all = both(third) + both(send(third, Y_LOW))

    fourth = jnp.where(own, fourth, send(fourth, TURN))
    fourth = ordered(fourth, send(fourth, CORE), core)
    fourth_all = collect(fourth)
    leaves = jnp.where(own, leaves, send(leaves, TURN))
    leaves = ordered(leaves, send(leaves, CORE), core)
    leaf_steps, leaf_far = ring(leaves, core)
    leaves_all = [leaves] + leaf_steps + [send(held, CORE) for held in leaf_steps] + [leaf_far]

    first = join(first, CORE, core)
    root = join(pivot_root[None], CORE, core)
    first = join(first, X_LOW, x_low)
    root = join(root, X_LOW, x_low)
    first = join(first, X_HIGH, x_high)
    root = join(root, X_HIGH, x_high)
    root = join(root, Y_HIGH, y_high)
    lowest = lax.dynamic_slice_in_dim(jnp.concatenate([first, root], axis=0), x_low * W, W, 2)
    lowest_all = four(jnp.stack(gathered(halves(lowest))))

    rows, high, low = path_rows(*fourth_all, *third_all, *second_all, *lowest_all)
    rows, far = lax.optimization_barrier((rows, leaves_all[-1]))
    leaves_all = leaves_all[:-1] + [far, send(far, CORE)]
    pairs, sides, leaf_high, leaf_low = pair_rows(rows, leaves_all)
    pairs = jnp.where(own, pairs, send(pairs, TURN))
    selves = self_rows(sides, high, low, leaf_high, leaf_low)
    selves = jnp.where(own, selves, send(selves, TURN))
    return pairs, pivot_leaves + selves


def solution(mesh):
    tree = P("pan", "sn")
    panel = P(None, "pan", "sn")
    return jax.shard_map(
        per_device,
        mesh=mesh,
        in_specs=(P(), tree, tree, panel, tree, panel, tree, panel, tree, panel, tree, panel),
        out_specs=(panel, tree),
        check_vma=False,
    )
```
